32 devices in a mesh: blk: 16 (over z, y, x), grp: 2 (over core).
Axes of the slice: x: 2, y: 2, z: 4, core: 2. Of those that a mesh axis runs over, the one named last changes fastest.
Arguments:
- image_emb: bfloat16 [4096, 1152], P(('blk', 'grp')), may hold values from -6 to 6
- text_feats: bfloat16 [4096, 640], P(('blk', 'grp')), may hold values from -6 to 6
- text_head: bfloat16 [640, 1152], replicated, may hold values from -0.25 to 0.25
Outputs:
- row_loss: float32 [4096], P(('blk', 'grp'))
- head_grad: float32 [640, 1152], P('blk')
The draws below stay inside these ranges and needn't reach their ends.
All inputs are finite; a program needn't handle non-finite values.
Results may differ from the reference program's by a relative error of at most 0.0053.
Values may be sent and summed in bfloat16 or wider, within the bound.
A program may use at most 64 MiB of HBM per device.

```python
import jax
import jax.numpy as jnp
from jax import lax

D = 640
E = 1152
TOK_DEV = 128
STEPS = 2
TOKENS = 4096
N_BLK = 16
N_GRP = 2


def strengthened(values, stream_key, source, target, parts, factor):
    def block_of(dim):
        return (jnp.arange(values.shape[dim]) // (values.shape[dim] // parts)).reshape((-1,) + (1,) * (values.ndim - 1 - dim))

    near = jax.random.permutation(stream_key, parts)[block_of(target)]
    second = (block_of(target) + parts // 2) % parts
    return jnp.where((block_of(source) == near) | (block_of(source) == second), factor * values, values)


def steps_of(rng, dims, cuts, smallest, high):
    level = 1.0
    for dim, blocks in cuts:
        heights = jax.random.uniform(jax.random.fold_in(jax.random.fold_in(rng, 6), dim), (blocks,), jnp.float32, smallest / len(cuts), high / len(cuts))
        level = level * jnp.repeat(jnp.exp(heights), dims[dim] // blocks).reshape((-1,) + (1,) * (len(dims) - 1 - dim))
    return level


def noise(key, extent, deviation, most, shards=(), held_as=jnp.bfloat16):
    values = jax.random.normal(key, extent, jnp.float32) * deviation
    if len(shards) > 0:
        values = steps_of(key, extent, shards, -0.22, 0.18) * values
    return jnp.clip(values, min=-most, max=most).astype(held_as)


def noise_with(key, shape, width, reach, split, heavy, kind=jnp.bfloat16):
    entries = width * jax.random.normal(key, shape, jnp.float32)
    if split:
        entries = entries * steps_of(key, shape, split, -0.22, 0.18)
    return jnp.clip(strengthened(entries, jax.random.fold_in(key, 3), *heavy), -reach, reach).astype(kind)


def setup_inputs(seed: int = 0) -> dict:
    key_of = jax.random.split(jax.random.key(seed), 4)
    image_emb = noise(key_of[0], (TOKENS, E), 1.0, 6.0, ((0, 32),))
    text_feats = noise_with(key_of[1], (TOKENS, D), 1.0, 6.0, ((0, 32),), (0, 1, 32, 2.75))
    text_head = noise(key_of[2], (D, E), D ** -0.5, 0.25)
    return {"image_emb": image_emb, "text_feats": text_feats, "text_head": text_head}


logit_scale = 20.0
logit_bias = -2.0
eps_norm = 1e-06

def reference(image_emb, text_feats, text_head):
    image_wide = image_emb.astype(jnp.float32)
    inverse = lax.rsqrt(lax.optimization_barrier(jnp.sum(image_wide * image_wide, axis=1, keepdims=True)) + eps_norm)
    images = (image_wide * inverse).astype(jnp.bfloat16)
    projected = jnp.dot(text_feats, text_head, preferred_element_type=jnp.float32)
    radius = jnp.sqrt(lax.optimization_barrier(jnp.sum(projected * projected, axis=1, keepdims=True)) + eps_norm)
    text_units = (projected / radius).astype(jnp.bfloat16)
    grid_shape = (N_BLK, N_GRP, TOK_DEV, E)
    image_grid = images.reshape(grid_shape).astype(jnp.float32)
    text_grid = text_units.reshape(grid_shape).astype(jnp.float32)
    pair_count = (STEPS + 1) * TOK_DEV
    identity = jnp.eye(TOK_DEV, dtype=jnp.float32)
    row_loss = jnp.zeros((N_BLK, N_GRP, TOK_DEV), jnp.float32)
    grad_text = jnp.zeros(grid_shape, jnp.float32)
    for hop_count in range(STEPS + 1):
        visitor = jnp.roll(text_grid, hop_count, axis=0)
        scores = logit_scale * jnp.einsum('bgie,bgje->bgij', image_grid, visitor) + logit_bias
        if hop_count == 0:
            pair_sign = 2.0 * identity - 1.0
        else:
            pair_sign = -jnp.ones((TOK_DEV, TOK_DEV), jnp.float32)
        margin_arg = -pair_sign * scores
        row_loss = row_loss + lax.optimization_barrier(jnp.sum(jax.nn.softplus(margin_arg), axis=3)) / pair_count
        pair_weight = (-pair_sign * jax.nn.sigmoid(margin_arg) * (logit_scale / pair_count)).astype(jnp.bfloat16)
        pair_weight = lax.optimization_barrier(pair_weight).astype(jnp.float32)
        partial_grad = jnp.einsum('bgij,bgie->bgje', pair_weight, image_grid)
        grad_text = grad_text + jnp.roll(partial_grad, -hop_count, axis=0)
    grad_flat = grad_text.reshape(TOKENS, E)
    along = lax.optimization_barrier(jnp.sum(projected * grad_flat, axis=1, keepdims=True))
    grad_proj = (grad_flat / radius - projected * (along / (radius * radius * radius))).astype(jnp.bfloat16)
    head_grad = jnp.dot(text_feats.T, grad_proj, preferred_element_type=jnp.float32)
    return (row_loss.reshape(TOKENS), head_grad)
```

```python
import functools

import jax
import jax.numpy as jnp
from jax import lax
from jax.experimental import pallas as pl
from jax.experimental.pallas import tpu as pltpu
from jax.sharding import PartitionSpec as P

STEPS = 2
MESH = pl.DeviceIdType.MESH

logit_scale = 20.0
logit_bias = -2.0
eps_norm = 1e-06

LANES = 128
N_CHUNK = 4
ORDERS = ((0, 1, 2, 3), (1, 2, 0, 3), (2, 0, 1, 3))


def position(order, dest):
    place = 0
    for bit in order:
        place = 2 * place + (dest >> bit) % 2
    return place


def unit_images(image_emb):
    wide = image_emb.astype(jnp.float32)
    inverse = lax.rsqrt(jnp.sum(wide * wide, axis=1, keepdims=True) + eps_norm)
    return (wide * inverse).astype(jnp.bfloat16)


def meet(images, feats, head, own):
    tok = images.shape[0]
    pairs = (STEPS + 1) * tok
    projected = jnp.dot(feats, head, preferred_element_type=jnp.float32)
    inverse = lax.rsqrt(jnp.sum(projected * projected, axis=1, keepdims=True) + eps_norm)
    texts = (projected * inverse).astype(jnp.bfloat16)
    scores = (
        logit_scale
        * lax.dot_general(texts, images, (((1,), (1,)), ((), ())), preferred_element_type=jnp.float32)
        + logit_bias
    )
    if own:
        same = lax.broadcasted_iota(jnp.int32, (tok, tok), 0) == lax.broadcasted_iota(
            jnp.int32, (tok, tok), 1
        )
        minus_sign = jnp.where(same, -1.0, 1.0)
        arg = minus_sign * scores
    else:
        arg = scores
    small = jnp.exp(-jnp.abs(arg))
    loss = jnp.sum(jnp.maximum(arg, 0.0) + jnp.log1p(small), axis=0, keepdims=True) / pairs
    weight = jnp.where(arg >= 0, 1.0, small) / (1.0 + small) * (logit_scale / pairs)
    if own:
        weight = minus_sign * weight
    grad = jnp.dot(weight.astype(jnp.bfloat16), images, preferred_element_type=jnp.float32)
    along = jnp.sum(projected * grad, axis=1, keepdims=True)
    grad_proj = inverse * (grad - projected * (along * inverse * inverse))
    return loss, grad_proj.astype(jnp.bfloat16)


def kernel(
    n_blk, image_hbm, feats_hbm, head_hbm, loss_ref, out_ref,
    image_v, head_v, units, feats, feats_t, grads, total, core_out, core_in,
    out0, out1, out2, out3, in0, in1, in2, in3, mine, theirs,
    load_sem, s1, r1, s2, r2, core_s, core_r, step_s, step_r, last_s, last_r,
):
    blk, grp = lax.axis_index("blk"), lax.axis_index("grp")
    parity = lax.rem(blk, 2)

    def flipped(bit):
        size = 1 << bit
        return blk + size * (1 - 2 * lax.rem(blk // size, 2))

    pair = (flipped(0), grp)
    ahead = (lax.rem(blk + 2, n_blk), grp)
    behind = (lax.rem(blk + n_blk - 2, n_blk), grp)
    other = (blk, 1 - grp)
    partners = [(flipped(bit), grp) for bit in range(4)]

    loads = [
        pltpu.make_async_copy(src, dst, load_sem.at[n])
        for n, (src, dst) in enumerate(((image_hbm, image_v), (feats_hbm, feats.at[0]), (head_hbm, head_v)))
    ]
    for load in loads:
        load.start()

    barrier = pltpu.get_barrier_semaphore()
    greeted = partners + [ahead, behind, other]
    for device in greeted:
        pl.semaphore_signal(barrier, inc=1, device_id=device, device_id_type=MESH)
    pl.semaphore_wait(barrier, len(greeted))

    def remote(src, dst, send, recv, device):
        return pltpu.make_async_remote_copy(
            src_ref=src, dst_ref=dst, send_sem=send, recv_sem=recv, device_id=device, device_id_type=MESH
        )

    rows = feats.shape[1] // N_CHUNK
    spans = [pl.ds(c * rows, rows) for c in range(N_CHUNK)]
    far = [
        remote(feats_hbm.at[w], feats.at[2, w], s2.at[c], r2.at[c], ahead) for c, w in enumerate(spans)
    ]
    near = [
        remote(feats_hbm.at[w], feats.at[1, w], s1.at[c], r1.at[c], pair) for c, w in enumerate(spans)
    ]
    onward = [
        remote(feats.at[2, w], feats.at[1, w], s1.at[c], r1.at[c], pair) for c, w in enumerate(spans)
    ]
    for copy in far:
        copy.start()

    @pl.when(parity == 0)
    def _():
        for copy in near:
            copy.start()

    loads[0].wait()
    units[...] = unit_images(image_v[...])
    loads[1].wait()
    loads[2].wait()

    tok = units.shape[0]

    def block(k):
        loss, grad = meet(units[...], feats[k], head_v[...], k == 0)
        grads[k * tok : (k + 1) * tok, :] = grad
        feats_t[:, k * tok : (k + 1) * tok] = feats[k].T
        return loss

    loss = block(0)

    for c in range(N_CHUNK):
        far[c].wait_recv()

        @pl.when(parity == 1)
        def _():
            onward[c].start()

    loss = loss + block(2)
    for copy in near:
        copy.wait_recv()
    loss_ref[...] = loss + block(1)

    depth = out_ref.shape[0]
    width = total.shape[2]
    columns = out_ref.shape[1] // len(ORDERS)
    tiles = columns // LANES
    full = depth * tiles
    first = grp == 0

    core_copies = [
        remote(core_out.at[p], core_in.at[p], core_s.at[p], core_r.at[p], other) for p in range(len(ORDERS))
    ]

    def products(p):
        grad = jnp.dot(
            feats_t[...], grads[:, p * columns : (p + 1) * columns], preferred_element_type=jnp.float32
        )
        for dest in range(n_blk):
            piece = grad[dest * depth : (dest + 1) * depth]
            stack = jnp.concatenate([piece[:, t * LANES : (t + 1) * LANES] for t in range(tiles)], axis=0)
            low, high = stack[:width], stack[full - width :]
            at = position(ORDERS[p], dest)
            total[p, at] = jnp.where(first, low, high)
            core_out[p, at] = jnp.where(first, high, low).astype(jnp.bfloat16)
        core_copies[p].start()

    outs, ins = (out0, out1, out2, out3), (in0, in1, in2, in3)
    step_copies = [
        [
            remote(outs[s].at[p], ins[s].at[p], step_s.at[p, s], step_r.at[p, s], partners[ORDERS[p][s]])
            for s in range(4)
        ]
        for p in range(len(ORDERS))
    ]
    base = [0] * len(ORDERS)

    def halve(p, s):
        count = n_blk >> (s + 1)
        bit = lax.rem(blk // (1 << ORDERS[p][s]), 2)
        keep, give = base[p] + bit * count, base[p] + (1 - bit) * count
        if s == 0:
            core_copies[p].wait_recv()
            arrived, start = core_in, 0
        else:
            step_copies[p][s - 1].wait_recv()
            arrived, start = ins[s - 1], base[p]
        gone = pl.ds(give, count)
        outs[s][p] = (total[p, gone] + arrived[p, pl.ds(give - start, count)].astype(jnp.float32)).astype(
            jnp.bfloat16
        )
        step_copies[p][s].start()
        stay = pl.ds(keep, count)
        total[p, stay] = total[p, stay] + arrived[p, pl.ds(keep - start, count)].astype(jnp.float32)
        base[p] = keep

    products(0)
    products(1)
    halve(0, 0)
    products(2)
    halve(1, 0)
    halve(2, 0)
    for s in range(1, 4):
        for p in range(len(ORDERS)):
            halve(p, s)
    for p in range(len(ORDERS)):
        step_copies[p][3].wait_recv()
        mine[p] = total[p, base[p]] + in3[p, 0].astype(jnp.float32)
    last = remote(mine, theirs, last_s, last_r, other)
    last.start()
    last.wait_recv()
    for p in range(len(ORDERS)):
        here, there = mine[p], theirs[p]
        low, high = jnp.where(first, here, there), jnp.where(first, there, here)
        stack = jnp.concatenate([low[: full - width], high], axis=0)
        for t in range(tiles):
            left = p * columns + t * LANES
            out_ref[:, left : left + LANES] = stack[t * depth : (t + 1) * depth]

    last.wait_send()
    for copy in far + near + core_copies:
        copy.wait_send()
    for chain in step_copies:
        for copy in chain:
            copy.wait_send()


def fused(n_blk, image_emb, text_feats, text_head):
    tok, emb = image_emb.shape
    feat = text_feats.shape[1]
    depth = feat // n_blk
    parts = len(ORDERS)
    full = depth * (emb // parts // LANES)
    width = (full // 2 + 15) // 16 * 16
    half = (parts, n_blk, width, LANES)
    steps = [pltpu.VMEM((parts, n_blk >> (s + 1), width, LANES), jnp.bfloat16) for s in range(4)]
    dma = pltpu.SemaphoreType.DMA
    loss, head_grad = pl.pallas_call(
        functools.partial(kernel, n_blk),
        out_shape=(
            jax.ShapeDtypeStruct((1, tok), jnp.float32),
            jax.ShapeDtypeStruct((depth, emb), jnp.float32),
        ),
        in_specs=[pl.BlockSpec(memory_space=pl.ANY)] * 3,
        out_specs=(pl.BlockSpec(memory_space=pltpu.VMEM),) * 2,
        scratch_shapes=[
            pltpu.VMEM((tok, emb), jnp.bfloat16),
            pltpu.VMEM((feat, emb), jnp.bfloat16),
            pltpu.VMEM((tok, emb), jnp.bfloat16),
            pltpu.VMEM((STEPS + 1, tok, feat), jnp.bfloat16),
            pltpu.VMEM((feat, (STEPS + 1) * tok), jnp.bfloat16),
            pltpu.VMEM(((STEPS + 1) * tok, emb), jnp.bfloat16),
            pltpu.VMEM(half, jnp.float32),
            pltpu.VMEM(half, jnp.bfloat16),
            pltpu.VMEM(half, jnp.bfloat16),
            *steps,
            *steps,
            pltpu.VMEM((parts, width, LANES), jnp.float32),
            pltpu.VMEM((parts, width, LANES), jnp.float32),
            dma((3,)),
            dma((N_CHUNK,)),
            dma((N_CHUNK,)),
            dma((N_CHUNK,)),
            dma((N_CHUNK,)),
            dma((parts,)),
            dma((parts,)),
            dma((parts, 4)),
            dma((parts, 4)),
            dma,
            dma,
        ],
        compiler_params=pltpu.CompilerParams(
            collective_id=0, has_side_effects=True, vmem_limit_bytes=40 * 1024 * 1024
        ),
    )(image_emb, text_feats, text_head)
    return loss.reshape(tok), head_grad


def shifted(block, axis, distance):
    n = lax.axis_size(axis)
    return lax.ppermute(block, axis, [((i - distance) % n, i) for i in range(n)])


def general(image_emb, text_feats, text_head):
    images = unit_images(image_emb)
    feats = [text_feats] + [shifted(text_feats, "blk", k) for k in range(1, STEPS + 1)]
    met = [meet(images, f, text_head, k == 0) for k, f in enumerate(feats)]
    loss = sum(m[0] for m in met).reshape(-1)
    local_grad = jnp.einsum(
        "td,te->de",
        jnp.concatenate(feats, axis=0),
        jnp.concatenate([m[1] for m in met], axis=0),
        preferred_element_type=jnp.float32,
    )
    row_sums = lax.psum_scatter(local_grad, "blk", scatter_dimension=0, tiled=True)
    return loss, lax.psum(row_sums, "grp")


def solution(mesh):
    n_blk, n_grp = mesh.shape["blk"], mesh.shape["grp"]
    body = functools.partial(fused, n_blk) if (n_blk, n_grp) == (16, 2) else general
    return jax.shard_map(
        body,
        mesh=mesh,
        in_specs=(P(("blk", "grp"), None), P(("blk", "grp"), None), P()),
        out_specs=(P(("blk", "grp")), P("blk", None)),
        check_vma=False,
    )
```

```python
import functools

import jax
import jax.numpy as jnp
from jax import lax
from jax.experimental import pallas as pl
from jax.experimental.pallas import tpu as pltpu
from jax.sharding import PartitionSpec as P

STEPS = 2
MESH = pl.DeviceIdType.MESH

logit_scale = 20.0
logit_bias = -2.0
eps_norm = 1e-06

LANES = 128
N_CHUNK = 4
STAGES = (((0, 1), (2, 3)), ((0, 1), (2, 3)), ((2, 3), (0, 1)))
ORDERS = tuple(sum(groups, ()) for groups in STAGES)
SUB = 1
CHAINS = SUB * len(ORDERS)


def position(order, dest):
    place = 0
    for bit in order:
        place = 2 * place + (dest >> bit) % 2
    return place


def unit_images(image_emb):
    wide = image_emb.astype(jnp.float32)
    inverse = lax.rsqrt(jnp.sum(wide * wide, axis=1, keepdims=True) + eps_norm)
    return (wide * inverse).astype(jnp.bfloat16)


def meet(images, feats, head, own):
    tok = images.shape[0]
    pairs = (STEPS + 1) * tok
    projected = jnp.dot(feats, head, preferred_element_type=jnp.float32)
    inverse = lax.rsqrt(jnp.sum(projected * projected, axis=1, keepdims=True) + eps_norm)
    texts = (projected * inverse).astype(jnp.bfloat16)
    scores = (
        logit_scale
        * lax.dot_general(texts, images, (((1,), (1,)), ((), ())), preferred_element_type=jnp.float32)
        + logit_bias
    )
    if own:
        same = lax.broadcasted_iota(jnp.int32, (tok, tok), 0) == lax.broadcasted_iota(
            jnp.int32, (tok, tok), 1
        )
        minus_sign = jnp.where(same, -1.0, 1.0)
        arg = minus_sign * scores
    else:
        arg = scores
    small = jnp.exp(-jnp.abs(arg))
    loss = jnp.sum(jnp.maximum(arg, 0.0) + jnp.log1p(small), axis=0, keepdims=True) / pairs
    weight = jnp.where(arg >= 0, 1.0, small) / (1.0 + small) * (logit_scale / pairs)
    if own:
        weight = minus_sign * weight
    grad = jnp.dot(weight.astype(jnp.bfloat16), images, preferred_element_type=jnp.float32)
    along = jnp.sum(projected * grad, axis=1, keepdims=True)
    grad_proj = inverse * (grad - projected * (along * inverse * inverse))
    return loss, grad_proj.astype(jnp.bfloat16)


def kernel(
    n_blk, image_hbm, feats_hbm, head_hbm, loss_ref, out_ref,
    image_v, head_v, units, feats, feats_t, grads, total, core_out, core_in,
    out0, out1, in0, in1, mine, theirs,
    load_sem, s1, r1, s2, r2, core_s, core_r, step_s, step_r, last_s, last_r,
):
    blk, grp = lax.axis_index("blk"), lax.axis_index("grp")
    parity = lax.rem(blk, 2)

    def flipped(bit):
        size = 1 << bit
        return blk + size * (1 - 2 * lax.rem(blk // size, 2))

    pair = (flipped(0), grp)
    ahead = (lax.rem(blk + 2, n_blk), grp)
    behind = (lax.rem(blk + n_blk - 2, n_blk), grp)
    other = (blk, 1 - grp)

    def bit_of(bit):
        return lax.rem(blk // (1 << bit), 2)

    def partner(group, mask):
        at = blk
        for n, bit in enumerate(group):
            if (mask >> n) % 2:
                at = at + (1 << bit) * (1 - 2 * bit_of(bit))
        return at, grp

    def share(group, mask):
        place = 0
        for n, bit in enumerate(group):
            value = bit_of(bit)
            place = 2 * place + (1 - value if (mask >> n) % 2 else value)
        return place

    partners = [partner(group, mask) for group in sorted({g for p in STAGES for g in p}) for mask in range(1, 1 << len(group))]

    loads = [
        pltpu.make_async_copy(src, dst, load_sem.at[n])
        for n, (src, dst) in enumerate(((image_hbm, image_v), (feats_hbm, feats.at[0]), (head_hbm, head_v)))
    ]
    for load in loads:
        load.start()

    barrier = pltpu.get_barrier_semaphore()
    greeted = partners + [ahead, behind, other]
    for device in greeted:
        pl.semaphore_signal(barrier, inc=1, device_id=device, device_id_type=MESH)
    pl.semaphore_wait(barrier, len(greeted))

    def remote(src, dst, send, recv, device):
        return pltpu.make_async_remote_copy(
            src_ref=src, dst_ref=dst, send_sem=send, recv_sem=recv, device_id=device, device_id_type=MESH
        )

    rows = feats.shape[1] // N_CHUNK
    spans = [pl.ds(c * rows, rows) for c in range(N_CHUNK)]
    far = [
        remote(feats_hbm.at[w], feats.at[2, w], s2.at[c], r2.at[c], ahead) for c, w in enumerate(spans)
    ]
    near = [
        remote(feats_hbm.at[w], feats.at[1, w], s1.at[c], r1.at[c], pair) for c, w in enumerate(spans)
    ]
    onward = [
        remote(feats.at[2, w], feats.at[1, w], s1.at[c], r1.at[c], pair) for c, w in enumerate(spans)
    ]
    for copy in far:
        copy.start()

    @pl.when(parity == 0)
    def _():
        for copy in near:
            copy.start()

    loads[0].wait()
    units[...] = unit_images(image_v[...])
    loads[1].wait()
    loads[2].wait()

    tok = units.shape[0]

    def block(k):
        loss, grad = meet(units[...], feats[k], head_v[...], k == 0)
        grads[k * tok : (k + 1) * tok, :] = grad
        feats_t[:, k * tok : (k + 1) * tok] = feats[k].T
        return loss

    loss = block(0)

    for c in range(N_CHUNK):
        far[c].wait_recv()

        @pl.when(parity == 1)
        def _():
            onward[c].start()

    loss = loss + block(2)
    for copy in near:
        copy.wait_recv()
    loss_ref[...] = loss + block(1)

    depth = out_ref.shape[0]
    short = total.shape[2]
    width = SUB * short
    columns = out_ref.shape[1] // len(ORDERS)
    tiles = columns // LANES
    full = depth * tiles
    first = grp == 0

    core_copies = [
        remote(core_out.at[q], core_in.at[q], core_s.at[q], core_r.at[q], other) for q in range(CHAINS)
    ]

    def products(p):
        grad = jnp.dot(
            feats_t[...], grads[:, p * columns : (p + 1) * columns], preferred_element_type=jnp.float32
        )
        for dest in range(n_blk):
            piece = grad[dest * depth : (dest + 1) * depth]
            stack = jnp.concatenate([piece[:, t * LANES : (t + 1) * LANES] for t in range(tiles)], axis=0)
            low, high = stack[:width], stack[full - width :]
            at = position(ORDERS[p], dest)
            kept = jnp.where(first, low, high)
            given = jnp.where(first, high, low).astype(jnp.bfloat16)
            for u in range(SUB):
                total[SUB * p + u, at] = kept[u * short : (u + 1) * short]
                core_out[SUB * p + u, at] = given[u * short : (u + 1) * short]
        for u in range(SUB):
            core_copies[SUB * p + u].start()

    outs, ins = (out0, out1), (in0, in1)

    def messages(q, s):
        group = STAGES[q // SUB][s]
        return [
            remote(
                outs[s].at[q, m - 1], ins[s].at[q, m - 1],
                step_s.at[q, s, m - 1], step_r.at[q, s, m - 1], partner(group, m),
            )
            for m in range(1, 1 << len(group))
        ]

    step_copies = [[messages(q, s) for s in range(2)] for q in range(CHAINS)]
    base = [0] * CHAINS
    count = [n_blk] * CHAINS

    def exchange(q, s):
        group = STAGES[q // SUB][s]
        start, size = base[q], count[q] >> len(group)
        if s == 0:
            core_copies[q].wait_recv()
        else:
            for copy in step_copies[q][s - 1]:
                copy.wait_recv()

        def summed(at):
            value = total[q, pl.ds(at, size)]
            if s == 0:
                return value + core_in[q, pl.ds(at, size)].astype(jnp.float32)
            for m in range(ins[s - 1].shape[1]):
                value = value + ins[s - 1][q, m, pl.ds(at - start, size)].astype(jnp.float32)
            return value

        for m, copy in reversed(list(enumerate(step_copies[q][s], 1))):
            outs[s][q, m - 1] = summed(start + share(group, m) * size).astype(jnp.bfloat16)
            copy.start()
        keep = start + share(group, 0) * size
        total[q, pl.ds(keep, size)] = summed(keep)
        base[q], count[q] = keep, size

    products(0)
    products(1)
    for u in range(SUB):
        exchange(u, 0)
    products(2)
    for q in range(SUB, CHAINS):
        exchange(q, 0)
    for q in range(CHAINS):
        exchange(q, 1)
    for q in range(CHAINS):
        for copy in step_copies[q][1]:
            copy.wait_recv()
        row = (q % SUB) * short
        value = total[q, base[q]]
        for m in range(in1.shape[1]):
            value = value + in1[q, m, 0].astype(jnp.float32)
        mine[q // SUB, row : row + short] = value
    last = remote(mine, theirs, last_s, last_r, other)
    last.start()
    last.wait_recv()
    for p in range(len(ORDERS)):
        here, there = mine[p], theirs[p]
        low, high = jnp.where(first, here, there), jnp.where(first, there, here)
        stack = jnp.concatenate([low[: full - width], high], axis=0)
        for t in range(tiles):
            left = p * columns + t * LANES
            out_ref[:, left : left + LANES] = stack[t * depth : (t + 1) * depth]

    last.wait_send()
    for copy in far + near + core_copies:
        copy.wait_send()
    for chain in step_copies:
        for copy in chain[0] + chain[1]:
            copy.wait_send()


def fused(n_blk, image_emb, text_feats, text_head):
    tok, emb = image_emb.shape
    feat = text_feats.shape[1]
    depth = feat // n_blk
    parts = len(ORDERS)
    full = depth * (emb // parts // LANES)
    unit = 16 * SUB
    width = (full // 2 + unit - 1) // unit * unit
    short = width // SUB
    half = (CHAINS, n_blk, short, LANES)
    steps = [pltpu.VMEM((CHAINS, 3, n_blk >> (2 * s + 2), short, LANES), jnp.bfloat16) for s in range(2)]
    dma = pltpu.SemaphoreType.DMA
    loss, head_grad = pl.pallas_call(
        functools.partial(kernel, n_blk),
        out_shape=(
            jax.ShapeDtypeStruct((1, tok), jnp.float32),
            jax.ShapeDtypeStruct((depth, emb), jnp.float32),
        ),
        in_specs=[pl.BlockSpec(memory_space=pltpu.HBM)] * 3,
        out_specs=(pl.BlockSpec(memory_space=pltpu.VMEM),) * 2,
        scratch_shapes=[
            pltpu.VMEM((tok, emb), jnp.bfloat16),
            pltpu.VMEM((feat, emb), jnp.bfloat16),
            pltpu.VMEM((tok, emb), jnp.bfloat16),
            pltpu.VMEM((STEPS + 1, tok, feat), jnp.bfloat16),
            pltpu.VMEM((feat, (STEPS + 1) * tok), jnp.bfloat16),
            pltpu.VMEM(((STEPS + 1) * tok, emb), jnp.bfloat16),
            pltpu.VMEM(half, jnp.float32),
            pltpu.VMEM(half, jnp.bfloat16),
            pltpu.VMEM(half, jnp.bfloat16),
            *steps,
            *steps,
            pltpu.VMEM((parts, width, LANES), jnp.float32),
            pltpu.VMEM((parts, width, LANES), jnp.float32),
            dma((3,)),
            dma((N_CHUNK,)),
            dma((N_CHUNK,)),
            dma((N_CHUNK,)),
            dma((N_CHUNK,)),
            dma((CHAINS,)),
            dma((CHAINS,)),
            dma((CHAINS, 2, 3)),
            dma((CHAINS, 2, 3)),
            dma,
            dma,
        ],
        compiler_params=pltpu.CompilerParams(
            collective_id=0, has_side_effects=True, vmem_limit_bytes=63 * 1024 * 1024
        ),
    )(image_emb, text_feats, text_head)
    return loss.reshape(tok), head_grad


def shifted(block, axis, distance):
    n = lax.axis_size(axis)
    return lax.ppermute(block, axis, [((i - distance) % n, i) for i in range(n)])


def general(image_emb, text_feats, text_head):
    images = unit_images(image_emb)
    feats = [text_feats] + [shifted(text_feats, "blk", k) for k in range(1, STEPS + 1)]
    met = [meet(images, f, text_head, k == 0) for k, f in enumerate(feats)]
    loss = sum(m[0] for m in met).reshape(-1)
    local_grad = jnp.einsum(
        "td,te->de",
        jnp.concatenate(feats, axis=0),
        jnp.concatenate([m[1] for m in met], axis=0),
        preferred_element_type=jnp.float32,
    )
    row_sums = lax.psum_scatter(local_grad, "blk", scatter_dimension=0, tiled=True)
    return loss, lax.psum(row_sums, "grp")


def solution(mesh):
    n_blk, n_grp = mesh.shape["blk"], mesh.shape["grp"]
    body = functools.partial(fused, n_blk) if (n_blk, n_grp) == (16, 2) else general
    return jax.shard_map(
        body,
        mesh=mesh,
        in_specs=(P(("blk", "grp"), None), P(("blk", "grp"), None), P()),
        out_specs=(P(("blk", "grp")), P("blk", None)),
        check_vma=False,
    )
```

```python
import functools

import jax
import jax.numpy as jnp
from jax import lax
from jax.experimental import pallas as pl
from jax.experimental.pallas import tpu as pltpu
from jax.sharding import PartitionSpec as P

STEPS = 2
MESH = pl.DeviceIdType.MESH

logit_scale = 20.0
logit_bias = -2.0
eps_norm = 1e-06

LANES = 128
N_CHUNK = 4
STAGES = (((0, 1), (2, 3)), ((0, 1), (2, 3)), ((2, 3), (0, 1)))
ORDERS = tuple(sum(groups, ()) for groups in STAGES)
SUB = 1
CHAINS = SUB * len(ORDERS)


def position(order, dest):
    place = 0
    for bit in order:
        place = 2 * place + (dest >> bit) % 2
    return place


def unit_images(image_emb):
    wide = image_emb.astype(jnp.float32)
    inverse = lax.rsqrt(jnp.sum(wide * wide, axis=1, keepdims=True) + eps_norm)
    return (wide * inverse).astype(jnp.bfloat16)


def meet(images, feats, head, own):
    tok = images.shape[0]
    pairs = (STEPS + 1) * tok
    projected = jnp.dot(feats, head, preferred_element_type=jnp.float32)
    inverse = lax.rsqrt(jnp.sum(projected * projected, axis=1, keepdims=True) + eps_norm)
    texts = (projected * inverse).astype(jnp.bfloat16)
    scores = (
        logit_scale
        * lax.dot_general(texts, images, (((1,), (1,)), ((), ())), preferred_element_type=jnp.float32)
        + logit_bias
    )
    if own:
        same = lax.broadcasted_iota(jnp.int32, (tok, tok), 0) == lax.broadcasted_iota(
            jnp.int32, (tok, tok), 1
        )
        minus_sign = jnp.where(same, -1.0, 1.0)
        arg = minus_sign * scores
    else:
        arg = scores
    small = jnp.exp(-jnp.abs(arg))
    loss = jnp.sum(jnp.maximum(arg, 0.0) + jnp.log1p(small), axis=0, keepdims=True) / pairs
    weight = jnp.where(arg >= 0, 1.0, small) / (1.0 + small) * (logit_scale / pairs)
    if own:
        weight = minus_sign * weight
    grad = jnp.dot(weight.astype(jnp.bfloat16), images, preferred_element_type=jnp.float32)
    along = jnp.sum(projected * grad, axis=1, keepdims=True)
    grad_proj = inverse * (grad - projected * (along * inverse * inverse))
    return loss, grad_proj.astype(jnp.bfloat16)


def kernel(
    n_blk, image_hbm, feats_hbm, head_hbm, loss_ref, out_ref,
    image_v, head_v, units, feats, feats_t, grads, early, total, core_out, core_in,
    out0, out1, in0, in1, mine, theirs,
    load_sem, s1, r1, s2, r2, core_s, core_r, step_s, step_r, last_s, last_r,
):
    blk, grp = lax.axis_index("blk"), lax.axis_index("grp")
    parity = lax.rem(blk, 2)

    def flipped(bit):
        size = 1 << bit
        return blk + size * (1 - 2 * lax.rem(blk // size, 2))

    pair = (flipped(0), grp)
    ahead = (lax.rem(blk + 2, n_blk), grp)
    behind = (lax.rem(blk + n_blk - 2, n_blk), grp)
    other = (blk, 1 - grp)

    def bit_of(bit):
        return lax.rem(blk // (1 << bit), 2)

    def partner(group, mask):
        at = blk
        for n, bit in enumerate(group):
            if (mask >> n) % 2:
                at = at + (1 << bit) * (1 - 2 * bit_of(bit))
        return at, grp

    def share(group, mask):
        place = 0
        for n, bit in enumerate(group):
            value = bit_of(bit)
            place = 2 * place + (1 - value if (mask >> n) % 2 else value)
        return place

    partners = [partner(group, mask) for group in sorted({g for p in STAGES for g in p}) for mask in range(1, 1 << len(group))]

    loads = [
        pltpu.make_async_copy(src, dst, load_sem.at[n])
        for n, (src, dst) in enumerate(((image_hbm, image_v), (feats_hbm, feats.at[0]), (head_hbm, head_v)))
    ]
    for load in loads:
        load.start()

    barrier = pltpu.get_barrier_semaphore()
    greeted = partners + [ahead, behind, other]
    for device in greeted:
        pl.semaphore_signal(barrier, inc=1, device_id=device, device_id_type=MESH)
    pl.semaphore_wait(barrier, len(greeted))

    def remote(src, dst, send, recv, device):
        return pltpu.make_async_remote_copy(
            src_ref=src, dst_ref=dst, send_sem=send, recv_sem=recv, device_id=device, device_id_type=MESH
        )

    rows = feats.shape[1] // N_CHUNK
    spans = [pl.ds(c * rows, rows) for c in range(N_CHUNK)]
    far = [
        remote(feats_hbm.at[w], feats.at[2, w], s2.at[c], r2.at[c], ahead) for c, w in enumerate(spans)
    ]
    near = [
        remote(feats_hbm.at[w], feats.at[1, w], s1.at[c], r1.at[c], pair) for c, w in enumerate(spans)
    ]
    onward = [
        remote(feats.at[2, w], feats.at[1, w], s1.at[c], r1.at[c], pair) for c, w in enumerate(spans)
    ]
    for copy in far:
        copy.start()

    @pl.when(parity == 0)
    def _():
        for copy in near:
            copy.start()

    loads[0].wait()
    units[...] = unit_images(image_v[...])
    loads[1].wait()
    loads[2].wait()

    tok = units.shape[0]

    def block(k):
        loss, grad = meet(units[...], feats[k], head_v[...], k == 0)
        at = (0, 2, 1)[k]
        grads[at * tok : (at + 1) * tok, :] = grad
        feats_t[:, at * tok : (at + 1) * tok] = feats[k].T
        return loss

    loss = block(0)

    for c in range(N_CHUNK):
        far[c].wait_recv()

        @pl.when(parity == 1)
        def _():
            onward[c].start()

    loss = loss + block(2)
    early[...] = jnp.dot(feats_t[:, : 2 * tok], grads[: 2 * tok], preferred_element_type=jnp.float32)
    for copy in near:
        copy.wait_recv()
    loss_ref[...] = loss + block(1)

    depth = out_ref.shape[0]
    short = total.shape[2]
    width = SUB * short
    columns = out_ref.shape[1] // len(ORDERS)
    tiles = columns // LANES
    full = depth * tiles
    first = grp == 0

    core_copies = [
        remote(core_out.at[q], core_in.at[q], core_s.at[q], core_r.at[q], other) for q in range(CHAINS)
    ]

    def products(p):
        span = slice(p * columns, (p + 1) * columns)
        grad = early[:, span] + jnp.dot(
            feats_t[:, 2 * tok :], grads[2 * tok :, span], preferred_element_type=jnp.float32
        )
        for dest in range(n_blk):
            piece = grad[dest * depth : (dest + 1) * depth]
            stack = jnp.concatenate([piece[:, t * LANES : (t + 1) * LANES] for t in range(tiles)], axis=0)
            low, high = stack[:width], stack[full - width :]
            at = position(ORDERS[p], dest)
            kept = jnp.where(first, low, high)
            given = jnp.where(first, high, low).astype(jnp.bfloat16)
            for u in range(SUB):
                total[SUB * p + u, at] = kept[u * short : (u + 1) * short]
                core_out[SUB * p + u, at] = given[u * short : (u + 1) * short]
        for u in range(SUB):
            core_copies[SUB * p + u].start()

    outs, ins = (out0, out1), (in0, in1)

    def messages(q, s):
        group = STAGES[q // SUB][s]
        return [
            remote(
                outs[s].at[q, m - 1], ins[s].at[q, m - 1],
                step_s.at[q, s, m - 1], step_r.at[q, s, m - 1], partner(group, m),
            )
            for m in range(1, 1 << len(group))
        ]

    step_copies = [[messages(q, s) for s in range(2)] for q in range(CHAINS)]
    base = [0] * CHAINS
    count = [n_blk] * CHAINS

    def exchange(q, s):
        group = STAGES[q // SUB][s]
        start, size = base[q], count[q] >> len(group)
        if s == 0:
            core_copies[q].wait_recv()
        else:
            for copy in step_copies[q][s - 1]:
                copy.wait_recv()

        def summed(at):
            value = total[q, pl.ds(at, size)]
            if s == 0:
                return value + core_in[q, pl.ds(at, size)].astype(jnp.float32)
            for m in range(ins[s - 1].shape[1]):
                value = value + ins[s - 1][q, m, pl.ds(at - start, size)].astype(jnp.float32)
            return value

        for m, copy in reversed(list(enumerate(step_copies[q][s], 1))):
            outs[s][q, m - 1] = summed(start + share(group, m) * size).astype(jnp.bfloat16)
            copy.start()
        keep = start + share(group, 0) * size
        total[q, pl.ds(keep, size)] = summed(keep)
        base[q], count[q] = keep, size

    products(0)
    products(1)
    for u in range(SUB):
        exchange(u, 0)
    products(2)
    for q in range(SUB, CHAINS):
        exchange(q, 0)
    for q in range(CHAINS):
        exchange(q, 1)
    for q in range(CHAINS):
        for copy in step_copies[q][1]:
            copy.wait_recv()
        row = (q % SUB) * short
        value = total[q, base[q]]
        for m in range(in1.shape[1]):
            value = value + in1[q, m, 0].astype(jnp.float32)
        mine[q // SUB, row : row + short] = value
    last = remote(mine, theirs, last_s, last_r, other)
    last.start()
    last.wait_recv()
    for p in range(len(ORDERS)):
        here, there = mine[p], theirs[p]
        low, high = jnp.where(first, here, there), jnp.where(first, there, here)
        stack = jnp.concatenate([low[: full - width], high], axis=0)
        for t in range(tiles):
            left = p * columns + t * LANES
            out_ref[:, left : left + LANES] = stack[t * depth : (t + 1) * depth]

    last.wait_send()
    for copy in far + near + core_copies:
        copy.wait_send()
    for chain in step_copies:
        for copy in chain[0] + chain[1]:
            copy.wait_send()


def fused(n_blk, image_emb, text_feats, text_head):
    tok, emb = image_emb.shape
    feat = text_feats.shape[1]
    depth = feat // n_blk
    parts = len(ORDERS)
    full = depth * (emb // parts // LANES)
    unit = 16 * SUB
    width = (full // 2 + unit - 1) // unit * unit
    short = width // SUB
    half = (CHAINS, n_blk, short, LANES)
    steps = [pltpu.VMEM((CHAINS, 3, n_blk >> (2 * s + 2), short, LANES), jnp.bfloat16) for s in range(2)]
    dma = pltpu.SemaphoreType.DMA
    loss, head_grad = pl.pallas_call(
        functools.partial(kernel, n_blk),
        out_shape=(
            jax.ShapeDtypeStruct((1, tok), jnp.float32),
            jax.ShapeDtypeStruct((depth, emb), jnp.float32),
        ),
        in_specs=[pl.BlockSpec(memory_space=pltpu.HBM)] * 3,
        out_specs=(pl.BlockSpec(memory_space=pltpu.VMEM),) * 2,
        scratch_shapes=[
            pltpu.VMEM((tok, emb), jnp.bfloat16),
            pltpu.VMEM((feat, emb), jnp.bfloat16),
            pltpu.VMEM((tok, emb), jnp.bfloat16),
            pltpu.VMEM((STEPS + 1, tok, feat), jnp.bfloat16),
            pltpu.VMEM((feat, (STEPS + 1) * tok), jnp.bfloat16),
            pltpu.VMEM(((STEPS + 1) * tok, emb), jnp.bfloat16),
            pltpu.VMEM((feat, emb), jnp.float32),
            pltpu.VMEM(half, jnp.float32),
            pltpu.VMEM(half, jnp.bfloat16),
            pltpu.VMEM(half, jnp.bfloat16),
            *steps,
            *steps,
            pltpu.VMEM((parts, width, LANES), jnp.float32),
            pltpu.VMEM((parts, width, LANES), jnp.float32),
            dma((3,)),
            dma((N_CHUNK,)),
            dma((N_CHUNK,)),
            dma((N_CHUNK,)),
            dma((N_CHUNK,)),
            dma((CHAINS,)),
            dma((CHAINS,)),
            dma((CHAINS, 2, 3)),
            dma((CHAINS, 2, 3)),
            dma,
            dma,
        ],
        compiler_params=pltpu.CompilerParams(
            collective_id=0, has_side_effects=True, vmem_limit_bytes=54784 * 1024
        ),
    )(image_emb, text_feats, text_head)
    return loss.reshape(tok), head_grad


def shifted(block, axis, distance):
    n = lax.axis_size(axis)
    return lax.ppermute(block, axis, [((i - distance) % n, i) for i in range(n)])


def general(image_emb, text_feats, text_head):
    images = unit_images(image_emb)
    feats = [text_feats] + [shifted(text_feats, "blk", k) for k in range(1, STEPS + 1)]
    met = [meet(images, f, text_head, k == 0) for k, f in enumerate(feats)]
    loss = sum(m[0] for m in met).reshape(-1)
    local_grad = jnp.einsum(
        "td,te->de",
        jnp.concatenate(feats, axis=0),
        jnp.concatenate([m[1] for m in met], axis=0),
        preferred_element_type=jnp.float32,
    )
    row_sums = lax.psum_scatter(local_grad, "blk", scatter_dimension=0, tiled=True)
    return loss, lax.psum(row_sums, "grp")


def solution(mesh):
    n_blk, n_grp = mesh.shape["blk"], mesh.shape["grp"]
    body = functools.partial(fused, n_blk) if (n_blk, n_grp) == (16, 2) else general
    return jax.shard_map(
        body,
        mesh=mesh,
        in_specs=(P(("blk", "grp"), None), P(("blk", "grp"), None), P()),
        out_specs=(P(("blk", "grp")), P("blk", None)),
        check_vma=False,
    )
```

```python
import functools

import jax
import jax.numpy as jnp
from jax import lax
from jax.experimental import pallas as pl
from jax.experimental.pallas import tpu as pltpu
from jax.sharding import PartitionSpec as P

STEPS = 2
MESH = pl.DeviceIdType.MESH

logit_scale = 20.0
logit_bias = -2.0
eps_norm = 1e-06

LANES = 128
N_CHUNK = 4
STAGES = (((0, 1), (2, 3)), ((0, 1), (2, 3)), ((2, 3), (0, 1)))
ORDERS = tuple(sum(groups, ()) for groups in STAGES)
SUB = 1
CHAINS = SUB * len(ORDERS)


def position(order, dest):
    place = 0
    for bit in order:
        place = 2 * place + (dest >> bit) % 2
    return place


def unit_images(image_emb):
    wide = image_emb.astype(jnp.float32)
    inverse = lax.rsqrt(jnp.sum(wide * wide, axis=1, keepdims=True) + eps_norm)
    return (wide * inverse).astype(jnp.bfloat16)


def meet(images, feats, head, own):
    tok = images.shape[0]
    pairs = (STEPS + 1) * tok
    projected = jnp.dot(feats, head, preferred_element_type=jnp.float32)
    inverse = lax.rsqrt(jnp.sum(projected * projected, axis=1, keepdims=True) + eps_norm)
    texts = (projected * inverse).astype(jnp.bfloat16)
    scores = (
        logit_scale
        * lax.dot_general(texts, images, (((1,), (1,)), ((), ())), preferred_element_type=jnp.float32)
        + logit_bias
    )
    if own:
        same = lax.broadcasted_iota(jnp.int32, (tok, tok), 0) == lax.broadcasted_iota(
            jnp.int32, (tok, tok), 1
        )
        minus_sign = jnp.where(same, -1.0, 1.0)
        arg = minus_sign * scores
    else:
        arg = scores
    small = jnp.exp(-jnp.abs(arg))
    loss = jnp.sum(jnp.maximum(arg, 0.0) + jnp.log1p(small), axis=0, keepdims=True) / pairs
    weight = jnp.where(arg >= 0, 1.0, small) / (1.0 + small) * (logit_scale / pairs)
    if own:
        weight = minus_sign * weight
    grad = jnp.dot(weight.astype(jnp.bfloat16), images, preferred_element_type=jnp.float32)
    along = jnp.sum(projected * grad, axis=1, keepdims=True)
    grad_proj = inverse * (grad - projected * (along * inverse * inverse))
    return loss, grad_proj.astype(jnp.bfloat16)


def kernel(
    n_blk, image_hbm, feats_hbm, head_hbm, loss_ref, out_ref,
    image_v, head_v, units, feats, feats_t, grads, early, total, core_out, core_in,
    out0, out1, in0, in1, mine, theirs,
    load_sem, s1, r1, s2, r2, core_s, core_r, step_s, step_r, last_s, last_r,
):
    blk, grp = lax.axis_index("blk"), lax.axis_index("grp")
    parity = lax.rem(blk, 2)

    def flipped(bit):
        size = 1 << bit
        return blk + size * (1 - 2 * lax.rem(blk // size, 2))

    pair = (flipped(0), grp)
    ahead = (lax.rem(blk + 2, n_blk), grp)
    behind = (lax.rem(blk + n_blk - 2, n_blk), grp)
    other = (blk, 1 - grp)

    def bit_of(bit):
        return lax.rem(blk // (1 << bit), 2)

    def partner(group, mask):
        at = blk
        for n, bit in enumerate(group):
            if (mask >> n) % 2:
                at = at + (1 << bit) * (1 - 2 * bit_of(bit))
        return at, grp

    def share(group, mask):
        place = 0
        for n, bit in enumerate(group):
            value = bit_of(bit)
            place = 2 * place + (1 - value if (mask >> n) % 2 else value)
        return place

    partners = [partner(group, mask) for group in sorted({g for p in STAGES for g in p}) for mask in range(1, 1 << len(group))]

    loads = [
        pltpu.make_async_copy(src, dst, load_sem.at[n])
        for n, (src, dst) in enumerate(((image_hbm, image_v), (feats_hbm, feats.at[0]), (head_hbm, head_v)))
    ]
    for load in loads:
        load.start()

    barrier = pltpu.get_barrier_semaphore()
    greeted = partners + [ahead, behind, other]
    for device in greeted:
        pl.semaphore_signal(barrier, inc=1, device_id=device, device_id_type=MESH)
    pl.semaphore_wait(barrier, len(greeted))

    def remote(src, dst, send, recv, device):
        return pltpu.make_async_remote_copy(
            src_ref=src, dst_ref=dst, send_sem=send, recv_sem=recv, device_id=device, device_id_type=MESH
        )

    rows = feats.shape[1] // N_CHUNK
    spans = [pl.ds(c * rows, rows) for c in range(N_CHUNK)]
    far = [
        remote(feats_hbm.at[w], feats.at[2, w], s2.at[c], r2.at[c], ahead) for c, w in enumerate(spans)
    ]
    near = [
        remote(feats_hbm.at[w], feats.at[1, w], s1.at[c], r1.at[c], pair) for c, w in enumerate(spans)
    ]
    onward = [
        remote(feats.at[2, w], feats.at[1, w], s1.at[c], r1.at[c], pair) for c, w in enumerate(spans)
    ]
    for copy in far:
        copy.start()

    @pl.when(parity == 0)
    def _():
        for copy in near:
            copy.start()

    loads[0].wait()
    units[...] = unit_images(image_v[...])
    loads[1].wait()
    loads[2].wait()

    tok = units.shape[0]

    def block(k):
        loss, grad = meet(units[...], feats[k], head_v[...], k == 0)
        at = (0, 2, 1)[k]
        grads[at * tok : (at + 1) * tok, :] = grad
        feats_t[:, at * tok : (at + 1) * tok] = feats[k].T
        return loss

    loss = block(0)

    for c in range(N_CHUNK):
        far[c].wait_recv()

        @pl.when(parity == 1)
        def _():
            onward[c].start()

    loss = loss + block(2)
    early[...] = jnp.dot(feats_t[:, : 2 * tok], grads[: 2 * tok], preferred_element_type=jnp.float32)
    for copy in near:
        copy.wait_recv()
    loss_ref[...] = loss + block(1)

    depth = out_ref.shape[0]
    short = total.shape[2]
    width = SUB * short
    columns = out_ref.shape[1] // len(ORDERS)
    tiles = columns // LANES
    full = depth * tiles
    first = grp == 0

    core_copies = [
        remote(core_out.at[q], core_in.at[q], core_s.at[q], core_r.at[q], other) for q in range(CHAINS)
    ]

    def products(p):
        span = slice(p * columns, (p + 1) * columns)
        grad = early[:, span] + jnp.dot(
            feats_t[:, 2 * tok :], grads[2 * tok :, span], preferred_element_type=jnp.float32
        )
        for dest in range(n_blk):
            piece = grad[dest * depth : (dest + 1) * depth]
            stack = jnp.concatenate([piece[:, t * LANES : (t + 1) * LANES] for t in range(tiles)], axis=0)
            low, high = stack[:width], stack[full - width :]
            at = position(ORDERS[p], dest)
            kept = jnp.where(first, low, high)
            given = jnp.where(first, high, low).astype(jnp.bfloat16)
            for u in range(SUB):
                total[SUB * p + u, at] = kept[u * short : (u + 1) * short]
                core_out[SUB * p + u, at] = given[u * short : (u + 1) * short]
        for u in range(SUB):
            core_copies[SUB * p + u].start()

    outs, ins = (out0, out1), (in0, in1)

    def messages(q, s):
        group = STAGES[q // SUB][s]
        return [
            remote(
                outs[s].at[q, m - 1], ins[s].at[q, m - 1],
                step_s.at[q, s, m - 1], step_r.at[q, s, m - 1], partner(group, m),
            )
            for m in range(1, 1 << len(group))
        ]

    step_copies = [[messages(q, s) for s in range(2)] for q in range(CHAINS)]
    base = [0] * CHAINS
    count = [n_blk] * CHAINS

    def exchange(q, s):
        group = STAGES[q // SUB][s]
        start, size = base[q], count[q] >> len(group)
        if s == 0:
            core_copies[q].wait_recv()
        else:
            for copy in step_copies[q][s - 1]:
                copy.wait_recv()

        def summed(at):
            value = total[q, pl.ds(at, size)]
            if s == 0:
                return value + core_in[q, pl.ds(at, size)].astype(jnp.float32)
            for m in range(ins[s - 1].shape[1]):
                value = value + ins[s - 1][q, m, pl.ds(at - start, size)].astype(jnp.float32)
            return value

        for m, copy in reversed(list(enumerate(step_copies[q][s], 1))):
            outs[s][q, m - 1] = summed(start + share(group, m) * size).astype(jnp.bfloat16)
            copy.start()
        keep = start + share(group, 0) * size
        total[q, pl.ds(keep, size)] = summed(keep)
        base[q], count[q] = keep, size

    products(2)
    products(0)
    products(1)
    for u in range(SUB):
        exchange(2 * SUB + u, 0)
    for u in range(SUB):
        exchange(u, 0)
    for q in range(SUB, 2 * SUB):
        exchange(q, 0)
    for q in range(CHAINS):
        exchange(q, 1)
    for q in range(CHAINS):
        for copy in step_copies[q][1]:
            copy.wait_recv()
        row = (q % SUB) * short
        value = total[q, base[q]]
        for m in range(in1.shape[1]):
            value = value + in1[q, m, 0].astype(jnp.float32)
        mine[q // SUB, row : row + short] = value
    last = remote(mine, theirs, last_s, last_r, other)
    last.start()
    last.wait_recv()
    for p in range(len(ORDERS)):
        here, there = mine[p], theirs[p]
        low, high = jnp.where(first, here, there), jnp.where(first, there, here)
        stack = jnp.concatenate([low[: full - width], high], axis=0)
        for t in range(tiles):
            left = p * columns + t * LANES
            out_ref[:, left : left + LANES] = stack[t * depth : (t + 1) * depth]

    last.wait_send()
    for copy in far + near + core_copies:
        copy.wait_send()
    for chain in step_copies:
        for copy in chain[0] + chain[1]:
            copy.wait_send()


def fused(n_blk, image_emb, text_feats, text_head):
    tok, emb = image_emb.shape
    feat = text_feats.shape[1]
    depth = feat // n_blk
    parts = len(ORDERS)
    full = depth * (emb // parts // LANES)
    unit = 16 * SUB
    width = (full // 2 + unit - 1) // unit * unit
    short = width // SUB
    half = (CHAINS, n_blk, short, LANES)
    steps = [pltpu.VMEM((CHAINS, 3, n_blk >> (2 * s + 2), short, LANES), jnp.bfloat16) for s in range(2)]
    dma = pltpu.SemaphoreType.DMA
    loss, head_grad = pl.pallas_call(
        functools.partial(kernel, n_blk),
        out_shape=(
            jax.ShapeDtypeStruct((1, tok), jnp.float32),
            jax.ShapeDtypeStruct((depth, emb), jnp.float32),
        ),
        in_specs=[pl.BlockSpec(memory_space=pltpu.HBM)] * 3,
        out_specs=(pl.BlockSpec(memory_space=pltpu.VMEM),) * 2,
        scratch_shapes=[
            pltpu.VMEM((tok, emb), jnp.bfloat16),
            pltpu.VMEM((feat, emb), jnp.bfloat16),
            pltpu.VMEM((tok, emb), jnp.bfloat16),
            pltpu.VMEM((STEPS + 1, tok, feat), jnp.bfloat16),
            pltpu.VMEM((feat, (STEPS + 1) * tok), jnp.bfloat16),
            pltpu.VMEM(((STEPS + 1) * tok, emb), jnp.bfloat16),
            pltpu.VMEM((feat, emb), jnp.float32),
            pltpu.VMEM(half, jnp.float32),
            pltpu.VMEM(half, jnp.bfloat16),
            pltpu.VMEM(half, jnp.bfloat16),
            *steps,
            *steps,
            pltpu.VMEM((parts, width, LANES), jnp.float32),
            pltpu.VMEM((parts, width, LANES), jnp.float32),
            dma((3,)),
            dma((N_CHUNK,)),
            dma((N_CHUNK,)),
            dma((N_CHUNK,)),
            dma((N_CHUNK,)),
            dma((CHAINS,)),
            dma((CHAINS,)),
            dma((CHAINS, 2, 3)),
            dma((CHAINS, 2, 3)),
            dma,
            dma,
        ],
        compiler_params=pltpu.CompilerParams(
            collective_id=0, has_side_effects=True, vmem_limit_bytes=54784 * 1024
        ),
    )(image_emb, text_feats, text_head)
    return loss.reshape(tok), head_grad


def shifted(block, axis, distance):
    n = lax.axis_size(axis)
    return lax.ppermute(block, axis, [((i - distance) % n, i) for i in range(n)])


def general(image_emb, text_feats, text_head):
    images = unit_images(image_emb)
    feats = [text_feats] + [shifted(text_feats, "blk", k) for k in range(1, STEPS + 1)]
    met = [meet(images, f, text_head, k == 0) for k, f in enumerate(feats)]
    loss = sum(m[0] for m in met).reshape(-1)
    local_grad = jnp.einsum(
        "td,te->de",
        jnp.concatenate(feats, axis=0),
        jnp.concatenate([m[1] for m in met], axis=0),
        preferred_element_type=jnp.float32,
    )
    row_sums = lax.psum_scatter(local_grad, "blk", scatter_dimension=0, tiled=True)
    return loss, lax.psum(row_sums, "grp")


def solution(mesh):
    n_blk, n_grp = mesh.shape["blk"], mesh.shape["grp"]
    body = functools.partial(fused, n_blk) if (n_blk, n_grp) == (16, 2) else general
    return jax.shard_map(
        body,
        mesh=mesh,
        in_specs=(P(("blk", "grp"), None), P(("blk", "grp"), None), P()),
        out_specs=(P(("blk", "grp")), P("blk", None)),
        check_vma=False,
    )
```

```python
import functools

import jax
import jax.numpy as jnp
from jax import lax
from jax.experimental import pallas as pl
from jax.experimental.pallas import tpu as pltpu
from jax.sharding import PartitionSpec as P

STEPS = 2
MESH = pl.DeviceIdType.MESH

logit_scale = 20.0
logit_bias = -2.0
eps_norm = 1e-06

LANES = 128
N_CHUNK = 4
STAGES = (((0, 1), (2, 3)), ((0, 1), (2, 3)), ((2, 3), (0, 1)))
ORDERS = tuple(sum(groups, ()) for groups in STAGES)
SUB = 1
CHAINS = SUB * len(ORDERS)


def position(order, dest):
    place = 0
    for bit in order:
        place = 2 * place + (dest >> bit) % 2
    return place


def unit_images(image_emb):
    wide = image_emb.astype(jnp.float32)
    inverse = lax.rsqrt(jnp.sum(wide * wide, axis=1, keepdims=True) + eps_norm)
    return (wide * inverse).astype(jnp.bfloat16)


def meet(images, feats, head, own):
    tok = images.shape[0]
    pairs = (STEPS + 1) * tok
    projected = jnp.dot(feats, head, preferred_element_type=jnp.float32)
    inverse = lax.rsqrt(jnp.sum(projected * projected, axis=1, keepdims=True) + eps_norm)
    texts = (projected * inverse).astype(jnp.bfloat16)
    scores = (
        logit_scale
        * lax.dot_general(texts, images, (((1,), (1,)), ((), ())), preferred_element_type=jnp.float32)
        + logit_bias
    )
    if own:
        same = lax.broadcasted_iota(jnp.int32, (tok, tok), 0) == lax.broadcasted_iota(
            jnp.int32, (tok, tok), 1
        )
        minus_sign = jnp.where(same, -1.0, 1.0)
        arg = minus_sign * scores
    else:
        arg = scores
    small = jnp.exp(-jnp.abs(arg))
    loss = jnp.sum(jnp.maximum(arg, 0.0) + jnp.log1p(small), axis=0, keepdims=True) / pairs
    weight = jnp.where(arg >= 0, 1.0, small) / (1.0 + small) * (logit_scale / pairs)
    if own:
        weight = minus_sign * weight
    grad = jnp.dot(weight.astype(jnp.bfloat16), images, preferred_element_type=jnp.float32)
    along = jnp.sum(projected * grad, axis=1, keepdims=True)
    grad_proj = inverse * (grad - projected * (along * inverse * inverse))
    return loss, grad_proj.astype(jnp.bfloat16)


def kernel(
    n_blk, image_hbm, feats_hbm, head_hbm, loss_ref, out_ref,
    image_v, head_v, units, feats, feats_t, grads, early, total, core_out, core_in,
    out0, out1, in0, in1, mine, theirs,
    load_sem, s1, r1, s2, r2, core_s, core_r, step_s, step_r, last_s, last_r,
):
    blk, grp = lax.axis_index("blk"), lax.axis_index("grp")
    parity = lax.rem(blk, 2)

    def flipped(bit):
        size = 1 << bit
        return blk + size * (1 - 2 * lax.rem(blk // size, 2))

    pair = (flipped(0), grp)
    ahead = (lax.rem(blk + 2, n_blk), grp)
    behind = (lax.rem(blk + n_blk - 2, n_blk), grp)
    other = (blk, 1 - grp)

    def bit_of(bit):
        return lax.rem(blk // (1 << bit), 2)

    def partner(group, mask):
        at = blk
        for n, bit in enumerate(group):
            if (mask >> n) % 2:
                at = at + (1 << bit) * (1 - 2 * bit_of(bit))
        return at, grp

    def share(group, mask):
        place = 0
        for n, bit in enumerate(group):
            value = bit_of(bit)
            place = 2 * place + (1 - value if (mask >> n) % 2 else value)
        return place

    partners = [partner(group, mask) for group in sorted({g for p in STAGES for g in p}) for mask in range(1, 1 << len(group))]

    loads = [
        pltpu.make_async_copy(src, dst, load_sem.at[n])
        for n, (src, dst) in enumerate(((image_hbm, image_v), (feats_hbm, feats.at[0]), (head_hbm, head_v)))
    ]
    for load in loads:
        load.start()

    barrier = pltpu.get_barrier_semaphore()
    greeted = partners + [ahead, behind, other]
    for device in greeted:
        pl.semaphore_signal(barrier, inc=1, device_id=device, device_id_type=MESH)
    pl.semaphore_wait(barrier, len(greeted))

    def remote(src, dst, send, recv, device):
        return pltpu.make_async_remote_copy(
            src_ref=src, dst_ref=dst, send_sem=send, recv_sem=recv, device_id=device, device_id_type=MESH
        )

    rows = feats.shape[1] // N_CHUNK
    spans = [pl.ds(c * rows, rows) for c in range(N_CHUNK)]
    far = [
        remote(feats_hbm.at[w], feats.at[2, w], s2.at[c], r2.at[c], ahead) for c, w in enumerate(spans)
    ]
    near = [
        remote(feats_hbm.at[w], feats.at[1, w], s1.at[c], r1.at[c], pair) for c, w in enumerate(spans)
    ]
    onward = [
        remote(feats.at[2, w], feats.at[1, w], s1.at[c], r1.at[c], pair) for c, w in enumerate(spans)
    ]
    for copy in far:
        copy.start()

    @pl.when(parity == 0)
    def _():
        for copy in near:
            copy.start()

    loads[0].wait()
    units[...] = unit_images(image_v[...])
    loads[1].wait()
    loads[2].wait()

    tok = units.shape[0]

    def block(k):
        loss, grad = meet(units[...], feats[k], head_v[...], k == 0)
        at = (0, 2, 1)[k]
        grads[at * tok : (at + 1) * tok, :] = grad
        feats_t[:, at * tok : (at + 1) * tok] = feats[k].T
        return loss

    loss = block(0)

    for c in range(N_CHUNK):
        far[c].wait_recv()

        @pl.when(parity == 1)
        def _():
            onward[c].start()

    loss = loss + block(2)
    early[...] = jnp.dot(feats_t[:, : 2 * tok], grads[: 2 * tok], preferred_element_type=jnp.float32)
    for copy in near:
        copy.wait_recv()
    loss_ref[...] = loss + block(1)

    depth = out_ref.shape[0]
    short = total.shape[2]
    width = SUB * short
    columns = out_ref.shape[1] // len(ORDERS)
    tiles = columns // LANES
    full = depth * tiles
    first = grp == 0

    core_copies = [
        remote(core_out.at[q], core_in.at[q], core_s.at[q], core_r.at[q], other) for q in range(CHAINS)
    ]

    def products(p):
        span = slice(p * columns, (p + 1) * columns)
        grad = early[:, span] + jnp.dot(
            feats_t[:, 2 * tok :], grads[2 * tok :, span], preferred_element_type=jnp.float32
        )
        for dest in range(n_blk):
            piece = grad[dest * depth : (dest + 1) * depth]
            stack = jnp.concatenate([piece[:, t * LANES : (t + 1) * LANES] for t in range(tiles)], axis=0)
            low, high = stack[:width], stack[full - width :]
            at = position(ORDERS[p], dest)
            kept = jnp.where(first, low, high)
            given = jnp.where(first, high, low).astype(jnp.bfloat16)
            for u in range(SUB):
                total[SUB * p + u, at] = kept[u * short : (u + 1) * short]
                core_out[SUB * p + u, at] = given[u * short : (u + 1) * short]
        for u in range(SUB):
            core_copies[SUB * p + u].start()

    outs, ins = (out0, out1), (in0, in1)

    def messages(q, s):
        group = STAGES[q // SUB][s]
        return [
            remote(
                outs[s].at[q, m - 1], ins[s].at[q, m - 1],
                step_s.at[q, s, m - 1], step_r.at[q, s, m - 1], partner(group, m),
            )
            for m in range(1, 1 << len(group))
        ]

    step_copies = [[messages(q, s) for s in range(2)] for q in range(CHAINS)]
    base = [0] * CHAINS
    count = [n_blk] * CHAINS

    def exchange(q, s):
        group = STAGES[q // SUB][s]
        start, size = base[q], count[q] >> len(group)
        if s == 0:
            core_copies[q].wait_recv()
        else:
            for copy in step_copies[q][s - 1]:
                copy.wait_recv()

        def summed(at):
            value = total[q, pl.ds(at, size)]
            if s == 0:
                return value + core_in[q, pl.ds(at, size)].astype(jnp.float32)
            for m in range(ins[s - 1].shape[1]):
                value = value + ins[s - 1][q, m, pl.ds(at - start, size)].astype(jnp.float32)
            return value

        for m, copy in reversed(list(enumerate(step_copies[q][s], 1))):
            outs[s][q, m - 1] = summed(start + share(group, m) * size).astype(jnp.bfloat16)
            copy.start()
        keep = start + share(group, 0) * size
        total[q, pl.ds(keep, size)] = summed(keep)
        base[q], count[q] = keep, size

    products(2)
    products(0)
    for u in range(SUB):
        exchange(2 * SUB + u, 0)
    products(1)
    for u in range(SUB):
        exchange(u, 0)
    for q in range(SUB, 2 * SUB):
        exchange(q, 0)
    for q in range(CHAINS):
        exchange(q, 1)
    for q in range(CHAINS):
        for copy in step_copies[q][1]:
            copy.wait_recv()
        row = (q % SUB) * short
        value = total[q, base[q]]
        for m in range(in1.shape[1]):
            value = value + in1[q, m, 0].astype(jnp.float32)
        mine[q // SUB, row : row + short] = value
    last = remote(mine, theirs, last_s, last_r, other)
    last.start()
    last.wait_recv()
    for p in range(len(ORDERS)):
        here, there = mine[p], theirs[p]
        low, high = jnp.where(first, here, there), jnp.where(first, there, here)
        stack = jnp.concatenate([low[: full - width], high], axis=0)
        for t in range(tiles):
            left = p * columns + t * LANES
            out_ref[:, left : left + LANES] = stack[t * depth : (t + 1) * depth]

    last.wait_send()
    for copy in far + near + core_copies:
        copy.wait_send()
    for chain in step_copies:
        for copy in chain[0] + chain[1]:
            copy.wait_send()


def fused(n_blk, image_emb, text_feats, text_head):
    tok, emb = image_emb.shape
    feat = text_feats.shape[1]
    depth = feat // n_blk
    parts = len(ORDERS)
    full = depth * (emb // parts // LANES)
    unit = 16 * SUB
    width = (full // 2 + unit - 1) // unit * unit
    short = width // SUB
    half = (CHAINS, n_blk, short, LANES)
    steps = [pltpu.VMEM((CHAINS, 3, n_blk >> (2 * s + 2), short, LANES), jnp.bfloat16) for s in range(2)]
    dma = pltpu.SemaphoreType.DMA
    loss, head_grad = pl.pallas_call(
        functools.partial(kernel, n_blk),
        out_shape=(
            jax.ShapeDtypeStruct((1, tok), jnp.float32),
            jax.ShapeDtypeStruct((depth, emb), jnp.float32),
        ),
        in_specs=[pl.BlockSpec(memory_space=pltpu.HBM)] * 3,
        out_specs=(pl.BlockSpec(memory_space=pltpu.VMEM),) * 2,
        scratch_shapes=[
            pltpu.VMEM((tok, emb), jnp.bfloat16),
            pltpu.VMEM((feat, emb), jnp.bfloat16),
            pltpu.VMEM((tok, emb), jnp.bfloat16),
            pltpu.VMEM((STEPS + 1, tok, feat), jnp.bfloat16),
            pltpu.VMEM((feat, (STEPS + 1) * tok), jnp.bfloat16),
            pltpu.VMEM(((STEPS + 1) * tok, emb), jnp.bfloat16),
            pltpu.VMEM((feat, emb), jnp.float32),
            pltpu.VMEM(half, jnp.float32),
            pltpu.VMEM(half, jnp.bfloat16),
            pltpu.VMEM(half, jnp.bfloat16),
            *steps,
            *steps,
            pltpu.VMEM((parts, width, LANES), jnp.float32),
            pltpu.VMEM((parts, width, LANES), jnp.float32),
            dma((3,)),
            dma((N_CHUNK,)),
            dma((N_CHUNK,)),
            dma((N_CHUNK,)),
            dma((N_CHUNK,)),
            dma((CHAINS,)),
            dma((CHAINS,)),
            dma((CHAINS, 2, 3)),
            dma((CHAINS, 2, 3)),
            dma,
            dma,
        ],
        compiler_params=pltpu.CompilerParams(
            collective_id=0, has_side_effects=True, vmem_limit_bytes=54784 * 1024
        ),
    )(image_emb, text_feats, text_head)
    return loss.reshape(tok), head_grad


def shifted(block, axis, distance):
    n = lax.axis_size(axis)
    return lax.ppermute(block, axis, [((i - distance) % n, i) for i in range(n)])


def general(image_emb, text_feats, text_head):
    images = unit_images(image_emb)
    feats = [text_feats] + [shifted(text_feats, "blk", k) for k in range(1, STEPS + 1)]
    met = [meet(images, f, text_head, k == 0) for k, f in enumerate(feats)]
    loss = sum(m[0] for m in met).reshape(-1)
    local_grad = jnp.einsum(
        "td,te->de",
        jnp.concatenate(feats, axis=0),
        jnp.concatenate([m[1] for m in met], axis=0),
        preferred_element_type=jnp.float32,
    )
    row_sums = lax.psum_scatter(local_grad, "blk", scatter_dimension=0, tiled=True)
    return loss, lax.psum(row_sums, "grp")


def solution(mesh):
    n_blk, n_grp = mesh.shape["blk"], mesh.shape["grp"]
    body = functools.partial(fused, n_blk) if (n_blk, n_grp) == (16, 2) else general
    return jax.shard_map(
        body,
        mesh=mesh,
        in_specs=(P(("blk", "grp"), None), P(("blk", "grp"), None), P()),
        out_specs=(P(("blk", "grp")), P("blk", None)),
        check_vma=False,
    )
```
